32 devices in a mesh: cases: 2 (over y), tm: 4 (over z), region: 4 (over x, core).
Axes of the slice: x: 2, y: 2, z: 4, core: 2. Of those that a mesh axis runs over, the one named last changes fastest.
Arguments:
- former_estimate: float32 [384, 32, 128], P(('cases', 'tm'), 'region'), parts along dimension 0, may hold values from -6 to 6
- excitation: bfloat16 [384, 32, 128], P(('cases', 'tm'), 'region'), parts along dimension 0, may hold values from -6 to 6
- susceptance_maps: bfloat16 [32, 4, 128, 128], P('region'), may hold values from -0.125 to 0.125
- linked_partner_target: int32 [32, 4], P('region'), may hold values from 0 to 31, as said below
- attenuation: float32 [32, 64], P('region'), may hold values from 0.0002 to 0.03
- revolution_angle: float32 [32, 64], P('region'), may hold values from -0.6 to 0.6
- saturated_flag: int32 [64, 64], P(('cases', 'region')), parts along dimension 0, may hold values 0 or 1
- gain_surge: float32 [384], P(('cases', 'tm')), parts along dimension 0, may hold values from 0.25 to 1
Outputs:
- waveform: float32 [384, 32, 128], P(('cases', 'tm'), 'region'), parts along dimension 0
The draws below stay inside these ranges and needn't reach their ends.
There are 2 independent parts, one for each index of `cases`. The reference program is written for one: setup_inputs(seed, part) draws one part's arguments, and reference() takes and returns one part's arrays. A program takes and returns all parts, laid end to end along the dimension named above; an argument that names none is the same for every part. Nothing has to cross between parts.
Inputs may be any that keep to these rules, and one draw needn't show every extreme that they name: `linked_partner_target`: block row b lies in region g = b // 8. Its column 0 is b itself, column 1 a block of region g, column 2 one of the last 4 blocks of region g - 1 and column 3 one of the first 4 blocks of region g + 1, regions counted around a cycle of 32 // 8.
All inputs are finite; a program needn't handle non-finite values. No bound on the sum of `saturated_flag` on one device may be relied on, other than what follows from the above.
Results may differ from the reference program's by a relative error of at most 0.0017.
Values may be sent and summed in bfloat16 or wider, within the bound.
A program may use at most 64 MiB of HBM per device.

```python
import math
import jax
import jax.numpy as jnp
from jax import lax

BUS = 64
BLK = 8
BND = 4
SWEEPS = 3
CLOCK_TICKS = 192
NB = 32


def draw_linked_partner_target(key, part):
    regions = NB // BLK
    rows = jnp.arange(NB, dtype=jnp.int32)
    home = rows // BLK
    key_inside, key_left, key_right = jax.random.split(key, 3)
    inside = home * BLK + jax.random.randint(key_inside, (NB,), 0, BLK)
    left_side = (home - 1) % regions * BLK + BLK - BND + jax.random.randint(key_left, (NB,), 0, BND)
    right_side = (home + 1) % regions * BLK + jax.random.randint(key_right, (NB,), 0, BND)
    return jnp.stack([rows, inside, left_side, right_side], axis=1).astype(jnp.int32)


def draw_gain_surge(key, part):
    where_key, depth_key = jax.random.split(key)
    flagged_positions = jax.random.randint(where_key, (4,), 0, CLOCK_TICKS)
    recursion_depth = jax.random.uniform(depth_key, (4,), jnp.float32, 0.5, 0.8)
    observation_moments = jnp.arange(CLOCK_TICKS)
    scaling_factor = jnp.ones((CLOCK_TICKS,), jnp.float32)
    for spike_ordinal in range(4):
        scaling_factor = scaling_factor * jnp.where(observation_moments == flagged_positions[spike_ordinal], recursion_depth[spike_ordinal], 1.0)
    return scaling_factor.astype(jnp.float32)


def place_ends(entries, own_key, low, high):
    extent = entries.shape
    index_at = [jax.random.randint(jax.random.fold_in(own_key, axis), (), 0, extent[axis]) for axis in range(len(extent))]
    entries = entries.at[tuple(index_at)].set(low)
    longest = extent.index(max(extent))
    index_at[longest] = (index_at[longest] + 1) % extent[longest]
    return entries.at[tuple(index_at)].set(high)


def levels(stream_key, shape, pieces, smallest, high):
    gain = 1.0
    for position, parts in pieces:
        steps = jax.random.uniform(jax.random.fold_in(jax.random.fold_in(stream_key, 6), position), (parts,), jnp.float32, smallest / len(pieces), high / len(pieces))
        gain = gain * jnp.repeat(jnp.exp(steps), shape[position] // parts).reshape((-1,) + (1,) * (len(shape) - 1 - position))
    return gain


def bell_draw(own_key, extent, deviation, most, cuts=(), kind=jnp.bfloat16):
    result = jax.random.normal(own_key, extent, jnp.float32) * deviation
    if len(cuts) > 0:
        result = levels(own_key, extent, cuts, -0.22, 0.18) * result
    return jnp.clip(result, min=-most, max=most).astype(kind)


def setup_inputs(seed: int = 0, part: int = 0) -> dict:
    splits = jax.random.split(jax.random.key(seed), 9)
    part_splits = jax.random.split(jax.random.fold_in(splits[8], part), 9)
    return {
        "former_estimate": bell_draw(part_splits[0], (CLOCK_TICKS, NB, 2 * BUS), 1.0, 6.0, ((0, 4), (1, 4)), jnp.float32),
        "excitation": bell_draw(part_splits[1], (CLOCK_TICKS, NB, 2 * BUS), 1.0, 6.0, ((0, 4), (1, 4))),
        "susceptance_maps": bell_draw(splits[2], (NB, 4, 2 * BUS, 2 * BUS), (32 * BUS) ** -0.5, 0.125, ((0, 4),)),
        "linked_partner_target": draw_linked_partner_target(jax.random.fold_in(splits[8], 71), part),
        "attenuation": jnp.clip(jnp.exp(math.log(0.03) - 5.0106353 * jax.random.uniform(splits[4], (NB, BUS), jnp.float32) ** levels(splits[4], (NB, BUS), ((0, 4),), -0.2, 0.2)), 0.0002, 0.03),
        "revolution_angle": jnp.clip(jax.random.uniform(splits[5], (NB, BUS), jnp.float32, -0.6, 0.6) * levels(splits[5], (NB, BUS), ((0, 4),), -0.4, 0.0), -0.6, 0.6),
        "saturated_flag": place_ends((jax.random.randint(part_splits[6], (NB, BUS), 0, 3) < 1).astype(jnp.int32), jax.random.fold_in(part_splits[6], 1), 0, 1),
        "gain_surge": draw_gain_surge(jax.random.fold_in(jax.random.fold_in(splits[8], part), 71), part),
    }


clip_level = 0.5

def complex_mul(first, second):
    half = first.shape[-1] // 2
    first_re, first_im = (first[..., :half], first[..., half:])
    second_re, second_im = (second[..., :half], second[..., half:])
    return jnp.concatenate([first_re * second_re - first_im * second_im, first_re * second_im + first_im * second_re], axis=-1)

def combine(early, late):
    return (complex_mul(late[0], early[0]), complex_mul(late[0], early[1]) + late[1])

def bus_terms(attenuation, revolution_angle):
    modulus = jnp.exp(-attenuation)
    cosine = modulus * jnp.cos(revolution_angle)
    sine = modulus * jnp.sin(revolution_angle)
    argument_spin = jnp.concatenate([cosine, sine], axis=-1)
    input_gain = jnp.sqrt((1.0 - cosine) ** 2 + sine ** 2)
    return (argument_spin, jnp.concatenate([input_gain, input_gain], axis=-1))

def limit_current(current, saturated_flag):
    half = current.shape[-1] // 2
    square = current[..., :half] ** 2 + current[..., half:] ** 2
    scaling_factor = jnp.where(saturated_flag == 1, clip_level / jnp.sqrt(clip_level ** 2 + square), 1.0)
    return current * jnp.concatenate([scaling_factor, scaling_factor], axis=-1)

def periodic_end(total_a, total_b):
    half = total_a.shape[-1] // 2
    denom_re = 1.0 - total_a[..., :half]
    denom_im = -total_a[..., half:]
    square = denom_re ** 2 + denom_im ** 2
    conjugate = jnp.concatenate([denom_re / square, -denom_im / square], axis=-1)
    return complex_mul(total_b, conjugate)

def reference(former_estimate, excitation, susceptance_maps, linked_partner_target, attenuation, revolution_angle, saturated_flag, gain_surge):
    argument_spin, input_gain = bus_terms(attenuation, revolution_angle)
    incremental_spin = gain_surge[:, None, None] * argument_spin[None]
    drive_base = excitation.astype(jnp.float32)
    wave = former_estimate
    for sweep_index in range(SWEEPS):
        rounded = wave.astype(jnp.bfloat16)
        current = jnp.zeros(wave.shape, jnp.float32)
        for column in range(4):
            picked = rounded[:, linked_partner_target[:, column], :].astype(jnp.float32)
            current = current + jnp.einsum('tbj,bij->tbi', picked, susceptance_maps[:, column].astype(jnp.float32))
        drive = input_gain[None] * (drive_base - limit_current(current, saturated_flag[None]))
        maps_a, maps_b = lax.associative_scan(combine, (incremental_spin, drive), axis=0)
        end_state = periodic_end(maps_a[-1], maps_b[-1])
        wave = complex_mul(maps_a, end_state[None]) + maps_b
    return wave
```

```python
import functools

import jax
import jax.numpy as jnp
from jax import lax
from jax.experimental import pallas as pl
from jax.experimental.pallas import tpu as pltpu
from jax.sharding import PartitionSpec as P

SWEEPS = 3
BND = 4
clip_level = 0.5
MESH = pl.DeviceIdType.MESH


def swap(v):
    return pltpu.roll(v, v.shape[-1] // 2, v.ndim - 1)


def dup(v):
    return jnp.concatenate([v, v], axis=-1)


def complex_pair(first, second):
    return (
        first[0] * second[0] - first[1] * second[1],
        first[0] * second[1] + first[1] * second[0],
    )


def dot_nt(x, w):
    return lax.dot_general(x, w, (((1,), (1,)), ((), ())), preferred_element_type=jnp.float32)


def kernel(
    n_tm,
    n_region,
    ticks,
    blocks,
    gain_ref,
    target_ref,
    former_ref,
    exc_ref,
    maps_ref,
    att_ref,
    angle_ref,
    flag_ref,
    out_ref,
    rounded,
    halo,
    sent_b,
    got_b,
    cur,
    scan_b,
    pow_re,
    pow_im,
    halo_re,
    halo_im,
    driven,
    driven_sw,
    spin,
    spin_near,
    gains,
    ends,
    ends_near,
    coef,
    halo_send,
    halo_recv,
    spin_send,
    spin_recv,
    gain_send,
    gain_recv,
    end_send,
    end_recv,
    near_send,
    near_recv,
):
    m = lax.axis_index("tm")
    r = lax.axis_index("region")
    right = lax.rem(r + 1, n_region)
    left = lax.rem(r + n_region - 1, n_region)
    sides = (left, right)
    width = out_ref.shape[-1]

    def rows(b):
        return pl.ds(b, ticks, stride=blocks)

    barrier = pltpu.get_barrier_semaphore()
    for k in range(n_tm):
        rank = lax.rem(m + k, n_tm)
        for region in (left, right) if k == 0 else (r, left, right):
            pl.semaphore_signal(
                barrier, inc=1, device_id={"tm": rank, "region": region}, device_id_type=MESH
            )

    lane = lax.broadcasted_iota(jnp.int32, (blocks, width), 1)
    row = lax.broadcasted_iota(jnp.int32, (blocks, width), 0)
    sign = jnp.where(lane < width // 2, -1.0, 1.0)
    upper = row < BND

    for b in range(blocks):
        rounded[b] = former_ref[rows(b), :].astype(jnp.bfloat16)
    modulus = jnp.exp(-dup(att_ref[...]))
    angle = dup(angle_ref[...])
    cosine = modulus * jnp.cos(angle)
    sine = modulus * jnp.sin(angle)
    gain_in = jnp.sqrt((1.0 - cosine) ** 2 + sine**2)
    spin_re = cosine
    spin_im = sign * sine
    spin[0] = spin_re
    spin[1] = spin_im
    total_gain = lax.fori_loop(0, ticks, lambda t, q: q * gain_ref[t], jnp.float32(1.0))
    gains[0] = jnp.full((blocks, width), total_gain, jnp.float32)

    pl.semaphore_wait(barrier, 3 * n_tm - 1)

    def halo_copies(step, src, dst):
        return [
            pltpu.make_async_remote_copy(
                src_ref=src.at[pl.ds(start, BND)],
                dst_ref=dst.at[pl.ds(start, BND)],
                send_sem=halo_send.at[step, side],
                recv_sem=halo_recv.at[step, side],
                device_id={"region": sides[side]},
                device_id_type=MESH,
            )
            for side, start in ((0, 0), (1, blocks - BND))
        ]

    first_halo = halo_copies(0, rounded, halo)
    spin_copies = [
        pltpu.make_async_remote_copy(
            src_ref=spin,
            dst_ref=spin_near.at[side],
            send_sem=spin_send.at[side],
            recv_sem=spin_recv.at[side],
            device_id={"region": sides[side]},
            device_id_type=MESH,
        )
        for side in range(2)
    ]
    gain_copies = [
        pltpu.make_async_remote_copy(
            src_ref=gains.at[0],
            dst_ref=gains.at[k],
            send_sem=gain_send.at[k],
            recv_sem=gain_recv.at[k],
            device_id={"tm": lax.rem(m + k, n_tm)},
            device_id_type=MESH,
        )
        for k in range(1, n_tm)
    ]
    pending = spin_copies + gain_copies
    for copy in first_halo + pending:
        copy.start()

    def partner(b, c):
        return lax.rem(target_ref[b, c], blocks)

    def own_part(b):
        x = jnp.concatenate([rounded[b], rounded[partner(b, 1)]], axis=1)
        return dot_nt(x, jnp.concatenate([maps_ref[b, 0], maps_ref[b, 1]], axis=1))

    def halo_part(b):
        x = jnp.concatenate([halo[partner(b, 2)], halo[partner(b, 3)]], axis=1)
        return dot_nt(x, jnp.concatenate([maps_ref[b, 2], maps_ref[b, 3]], axis=1))

    for b in range(blocks):
        cur[rows(b), :] = own_part(b)

    exc = exc_ref[...].astype(jnp.float32).reshape(ticks, blocks, width)
    exc = exc * gain_in[None]
    driven[...] = exc.reshape(ticks * blocks, width)
    driven_sw[...] = swap(driven[...])

    def powers(base_re, base_im, to_re, to_im):
        def step(t, carry):
            q, re, im = carry
            q = q * gain_ref[t]
            re, im = complex_pair((re, im), (base_re, base_im))
            at = pl.ds(pl.multiple_of(t * blocks, blocks), blocks)
            to_re[at, :] = q * re
            to_im[at, :] = q * im
            return q, re, im

        one = jnp.ones((blocks, width), jnp.float32)
        _, re, im = lax.fori_loop(
            0, ticks, step, (jnp.float32(1.0), one, jnp.zeros_like(one)), unroll=8
        )
        return re, im

    def coefficients(full, base):
        one = (jnp.ones((blocks, width), jnp.float32), jnp.zeros((blocks, width), jnp.float32))
        after, within = one, one
        for j in reversed(range(n_tm)):
            k = lax.rem(m - j + n_tm, n_tm)
            before = j < m
            factor = gains[k]
            end = (factor * full[0], factor * full[1])
            coef[base, k, 0] = after[0]
            coef[base, k, 1] = after[1]
            coef[base, k, 2] = jnp.where(before, within[0], 0.0)
            coef[base, k, 3] = jnp.where(before, within[1], 0.0)
            after = complex_pair(after, end)
            longer = complex_pair(within, end)
            within = tuple(jnp.where(before, a, b) for a, b in zip(longer, within))
        down = (1.0 - after[0], -after[1])
        square = down[0] ** 2 + down[1] ** 2
        head = complex_pair(within, (down[0] / square, -down[1] / square))
        for k in range(n_tm):
            c = complex_pair(head, (coef[base, k, 0], coef[base, k, 1]))
            coef[base, k, 0] = c[0] + coef[base, k, 2]
            coef[base, k, 1] = c[1] + coef[base, k, 3]

    own_full = powers(spin_re, spin_im, pow_re, pow_im)
    for copy in spin_copies + gain_copies:
        copy.wait_recv()
    coefficients(own_full, 0)
    near_re = jnp.where(upper, spin_near[0, 0], spin_near[1, 0])
    near_im = jnp.where(upper, spin_near[0, 1], spin_near[1, 1])
    halo_full = powers(near_re, near_im, halo_re, halo_im)
    coefficients(halo_full, 1)

    limited = dup(flag_ref[...]) == 1

    for copy in first_halo:
        copy.wait_recv()
    for b in range(blocks):
        cur[rows(b), :] += halo_part(b)

    for sweep in range(SWEEPS):

        def scan_step(t, carry):
            s, z = carry
            at = pl.ds(pl.multiple_of(t * blocks, blocks), blocks)
            c = cur[at, :]
            c_sw = swap(c)
            scale = jnp.where(
                limited,
                gain_in * (clip_level * lax.rsqrt(clip_level**2 + (c * c + c_sw * c_sw))),
                gain_in,
            )
            g = gain_ref[t]
            a_re = g * spin_re
            a_im = g * spin_im
            new_s = a_re * s + (a_im * z + (driven[at, :] - scale * c))
            new_z = a_re * z + ((driven_sw[at, :] - scale * c_sw) - a_im * s)
            scan_b[at, :] = new_s
            return new_s, new_z

        zero = jnp.zeros((blocks, width), jnp.float32)
        end_b, _ = lax.fori_loop(0, ticks, scan_step, (zero, zero), unroll=12)
        last = sweep == SWEEPS - 1
        ends[sweep, 0] = end_b
        end_copies = [
            pltpu.make_async_remote_copy(
                src_ref=ends.at[sweep, 0],
                dst_ref=ends.at[sweep, k],
                send_sem=end_send.at[sweep, k],
                recv_sem=end_recv.at[sweep, k],
                device_id={"tm": lax.rem(m + k, n_tm)},
                device_id_type=MESH,
            )
            for k in range(1, n_tm)
        ]
        near_copies = []
        halo_b = []
        if not last:
            near_copies = [
                pltpu.make_async_remote_copy(
                    src_ref=ends.at[sweep, 0],
                    dst_ref=ends_near.at[sweep, side, k],
                    send_sem=near_send.at[sweep, side, k],
                    recv_sem=near_recv.at[sweep, side, k],
                    device_id={"tm": lax.rem(m + k, n_tm), "region": sides[side]},
                    device_id_type=MESH,
                )
                for k in range(n_tm)
                for side in range(2)
            ]
            halo_b = halo_copies(sweep + 1, sent_b.at[sweep], got_b.at[sweep])
        for copy in end_copies + near_copies:
            copy.start()
        if not last:
            for b in range(blocks):
                sent_b[sweep, b] = scan_b[rows(b), :].astype(jnp.bfloat16)
            for copy in halo_b:
                copy.start()
        pending += end_copies + near_copies + halo_b

        def start_state(base, end_of):
            state = jnp.zeros((blocks, width), jnp.float32)
            for k in range(n_tm):
                v = end_of(k)
                state += coef[base, k, 0] * v + coef[base, k, 1] * swap(v)
            return state, swap(state)

        for copy in end_copies:
            copy.wait_recv()
        state, state_sw = start_state(0, lambda k: ends[sweep, k])
        if last:
            shape = (ticks, blocks, width)
            out = (
                pow_re[...].reshape(shape) * state[None]
                + pow_im[...].reshape(shape) * state_sw[None]
                + scan_b[...].reshape(shape)
            )
            out_ref[...] = out.reshape(ticks * blocks, width)
        else:
            if sweep == 0:
                for copy in first_halo:
                    copy.wait_send()
            for b in range(blocks):
                rounded[b] = (
                    pow_re[rows(b), :] * state[b : b + 1]
                    + pow_im[rows(b), :] * state_sw[b : b + 1]
                    + scan_b[rows(b), :]
                ).astype(jnp.bfloat16)
            for b in range(blocks):
                cur[rows(b), :] = own_part(b)
            for copy in near_copies:
                copy.wait_recv()
            state, state_sw = start_state(
                1,
                lambda k: jnp.where(upper, ends_near[sweep, 0, k], ends_near[sweep, 1, k]),
            )
            for copy in halo_b:
                copy.wait_recv()
            for b in range(blocks):
                halo[b] = (
                    halo_re[rows(b), :] * state[b : b + 1]
                    + halo_im[rows(b), :] * state_sw[b : b + 1]
                    + got_b[sweep, b].astype(jnp.float32)
                ).astype(jnp.bfloat16)
            for b in range(blocks):
                cur[rows(b), :] += halo_part(b)
    for copy in pending:
        copy.wait_send()


def local(n_tm, n_region, former, excitation, maps, target, attenuation, angle, flag, gain):
    ticks, blocks, width = former.shape
    flat = (ticks * blocks, width)
    f32, bf16 = jnp.float32, jnp.bfloat16
    rounds = SWEEPS - 1
    vmem = pl.BlockSpec(memory_space=pltpu.VMEM)
    smem = pl.BlockSpec(memory_space=pltpu.SMEM)
    dma = pltpu.SemaphoreType.DMA
    out = pl.pallas_call(
        functools.partial(kernel, n_tm, n_region, ticks, blocks),
        out_shape=jax.ShapeDtypeStruct(flat, f32),
        in_specs=[smem, smem] + [vmem] * 6,
        out_specs=vmem,
        scratch_shapes=[
            pltpu.VMEM((blocks, ticks, width), bf16),
            pltpu.VMEM((blocks, ticks, width), bf16),
            pltpu.VMEM((rounds, blocks, ticks, width), bf16),
            pltpu.VMEM((rounds, blocks, ticks, width), bf16),
            pltpu.VMEM(flat, f32),
            pltpu.VMEM(flat, f32),
            pltpu.VMEM(flat, f32),
            pltpu.VMEM(flat, f32),
            pltpu.VMEM(flat, f32),
            pltpu.VMEM(flat, f32),
            pltpu.VMEM(flat, f32),
            pltpu.VMEM(flat, f32),
            pltpu.VMEM((2, blocks, width), f32),
            pltpu.VMEM((2, 2, blocks, width), f32),
            pltpu.VMEM((n_tm, blocks, width), f32),
            pltpu.VMEM((SWEEPS, n_tm, blocks, width), f32),
            pltpu.VMEM((rounds, 2, n_tm, blocks, width), f32),
            pltpu.VMEM((2, n_tm, 4, blocks, width), f32),
            dma((SWEEPS, 2)),
            dma((SWEEPS, 2)),
            dma((2,)),
            dma((2,)),
            dma((n_tm,)),
            dma((n_tm,)),
            dma((SWEEPS, n_tm)),
            dma((SWEEPS, n_tm)),
            dma((rounds, 2, n_tm)),
            dma((rounds, 2, n_tm)),
        ],
        compiler_params=pltpu.CompilerParams(
            collective_id=0, has_side_effects=True, vmem_limit_bytes=40 * 2**20
        ),
        name="picard",
    )(
        gain,
        target,
        former.reshape(flat),
        excitation.reshape(flat),
        maps,
        attenuation,
        angle,
        flag,
    )
    return out.reshape(ticks, blocks, width)


def solution(mesh):
    in_specs = (
        P(("cases", "tm"), "region", None),
        P(("cases", "tm"), "region", None),
        P("region", None, None, None),
        P("region", None),
        P("region", None),
        P("region", None),
        P(("cases", "region"), None),
        P(("cases", "tm")),
    )
    return jax.shard_map(
        functools.partial(local, mesh.shape["tm"], mesh.shape["region"]),
        mesh=mesh,
        in_specs=in_specs,
        out_specs=P(("cases", "tm"), "region", None),
        check_vma=False,
    )
```

```python
import functools

import jax
import jax.numpy as jnp
from jax import lax
from jax.experimental import pallas as pl
from jax.experimental.pallas import tpu as pltpu
from jax.sharding import PartitionSpec as P

SWEEPS = 3
BND = 4
clip_level = 0.5
MESH = pl.DeviceIdType.MESH


def swap(v):
    return pltpu.roll(v, v.shape[-1] // 2, v.ndim - 1)


def dup(v):
    return jnp.concatenate([v, v], axis=-1)


def complex_pair(first, second):
    return (
        first[0] * second[0] - first[1] * second[1],
        first[0] * second[1] + first[1] * second[0],
    )


def dot_nt(x, w):
    return lax.dot_general(x, w, (((1,), (1,)), ((), ())), preferred_element_type=jnp.float32)


def kernel(
    n_tm,
    n_region,
    ticks,
    blocks,
    gain_hbm,
    target_hbm,
    former_hbm,
    exc_hbm,
    maps_hbm,
    att_hbm,
    angle_hbm,
    flag_hbm,
    out_ref,
    gain_ref,
    target_ref,
    former_ref,
    exc_ref,
    maps_ref,
    att_ref,
    angle_ref,
    flag_ref,
    rounded,
    halo,
    sent_b,
    got_b,
    cur,
    scan_b,
    pow_re,
    pow_im,
    halo_re,
    halo_im,
    driven,
    driven_sw,
    drive,
    drive_sw,
    spin,
    spin_near,
    gains,
    ends,
    ends_near,
    coef,
    halo_send,
    halo_recv,
    spin_send,
    spin_recv,
    gain_send,
    gain_recv,
    end_send,
    end_recv,
    near_send,
    near_recv,
    fetch_sem,
):
    m = lax.axis_index("tm")
    r = lax.axis_index("region")
    right = lax.rem(r + 1, n_region)
    left = lax.rem(r + n_region - 1, n_region)
    sides = (left, right)
    width = out_ref.shape[-1]

    def rows(b):
        return pl.ds(b, ticks, stride=blocks)

    fetches = [
        pltpu.make_async_copy(src, dst, fetch_sem.at[i])
        for i, (src, dst) in enumerate(
            (
                (former_hbm, former_ref),
                (att_hbm, att_ref),
                (angle_hbm, angle_ref),
                (gain_hbm, gain_ref),
                (target_hbm, target_ref),
                (maps_hbm, maps_ref),
                (exc_hbm, exc_ref),
                (flag_hbm, flag_ref),
            )
        )
    ]
    for fetch in fetches:
        fetch.start()
    barrier = pltpu.get_barrier_semaphore()
    for k in range(n_tm):
        rank = lax.rem(m + k, n_tm)
        for region in (left, right) if k == 0 else (r, left, right):
            pl.semaphore_signal(
                barrier, inc=1, device_id={"tm": rank, "region": region}, device_id_type=MESH
            )

    lane = lax.broadcasted_iota(jnp.int32, (blocks, width), 1)
    row = lax.broadcasted_iota(jnp.int32, (blocks, width), 0)
    sign = jnp.where(lane < width // 2, -1.0, 1.0)
    upper = row < BND

    fetches[0].wait()
    for b in range(blocks):
        rounded[b] = former_ref[rows(b), :].astype(jnp.bfloat16)
    for fetch in fetches[1:4]:
        fetch.wait()
    modulus = jnp.exp(-dup(att_ref[...]))
    angle = dup(angle_ref[...])
    cosine = modulus * jnp.cos(angle)
    sine = modulus * jnp.sin(angle)
    gain_in = jnp.sqrt((1.0 - cosine) ** 2 + sine**2)
    spin_re = cosine
    spin_im = sign * sine
    spin[0] = spin_re
    spin[1] = spin_im
    total_gain = lax.fori_loop(0, ticks, lambda t, q: q * gain_ref[t], jnp.float32(1.0))
    gains[0] = jnp.full((blocks, width), total_gain, jnp.float32)

    def partner(b, c):
        return lax.rem(target_ref[c, b], blocks)

    def own_part(b):
        x = jnp.concatenate([rounded[b], rounded[partner(b, 1)]], axis=1)
        return dot_nt(x, jnp.concatenate([maps_ref[b, 0], maps_ref[b, 1]], axis=1))

    def halo_part(b):
        x = jnp.concatenate([halo[partner(b, 2)], halo[partner(b, 3)]], axis=1)
        return dot_nt(x, jnp.concatenate([maps_ref[b, 2], maps_ref[b, 3]], axis=1))

    for fetch in fetches[4:]:
        fetch.wait()
    for b in range(blocks):
        cur[rows(b), :] = own_part(b)

    exc = exc_ref[...].astype(jnp.float32).reshape(ticks, blocks, width)
    exc = exc * gain_in[None]
    driven[...] = exc.reshape(ticks * blocks, width)
    driven_sw[...] = swap(driven[...])

    def powers(base_re, base_im, to_re, to_im):
        def step(t, carry):
            q, re, im = carry
            q = q * gain_ref[t]
            re, im = complex_pair((re, im), (base_re, base_im))
            at = pl.ds(pl.multiple_of(t * blocks, blocks), blocks)
            to_re[at, :] = q * re
            to_im[at, :] = q * im
            return q, re, im

        one = jnp.ones((blocks, width), jnp.float32)
        _, re, im = lax.fori_loop(
            0, ticks, step, (jnp.float32(1.0), one, jnp.zeros_like(one)), unroll=True
        )
        return re, im

    def coefficients(full, base):
        one = (jnp.ones((blocks, width), jnp.float32), jnp.zeros((blocks, width), jnp.float32))
        after, within = one, one
        for j in reversed(range(n_tm)):
            k = lax.rem(m - j + n_tm, n_tm)
            before = j < m
            factor = gains[k]
            end = (factor * full[0], factor * full[1])
            coef[base, k, 0] = after[0]
            coef[base, k, 1] = after[1]
            coef[base, k, 2] = jnp.where(before, within[0], 0.0)
            coef[base, k, 3] = jnp.where(before, within[1], 0.0)
            after = complex_pair(after, end)
            longer = complex_pair(within, end)
            within = tuple(jnp.where(before, a, b) for a, b in zip(longer, within))
        down = (1.0 - after[0], -after[1])
        square = down[0] ** 2 + down[1] ** 2
        head = complex_pair(within, (down[0] / square, -down[1] / square))
        for k in range(n_tm):
            c = complex_pair(head, (coef[base, k, 0], coef[base, k, 1]))
            coef[base, k, 0] = c[0] + coef[base, k, 2]
            coef[base, k, 1] = c[1] + coef[base, k, 3]

    own_full = powers(spin_re, spin_im, pow_re, pow_im)
    pl.semaphore_wait(barrier, 3 * n_tm - 1)

    def halo_copies(step, src, dst):
        return [
            pltpu.make_async_remote_copy(
                src_ref=src.at[pl.ds(start, BND)],
                dst_ref=dst.at[pl.ds(start, BND)],
                send_sem=halo_send.at[step, side],
                recv_sem=halo_recv.at[step, side],
                device_id={"region": sides[side]},
                device_id_type=MESH,
            )
            for side, start in ((0, 0), (1, blocks - BND))
        ]

    first_halo = halo_copies(0, rounded, halo)
    spin_copies = [
        pltpu.make_async_remote_copy(
            src_ref=spin,
            dst_ref=spin_near.at[side],
            send_sem=spin_send.at[side],
            recv_sem=spin_recv.at[side],
            device_id={"region": sides[side]},
            device_id_type=MESH,
        )
        for side in range(2)
    ]
    gain_copies = [
        pltpu.make_async_remote_copy(
            src_ref=gains.at[0],
            dst_ref=gains.at[k],
            send_sem=gain_send.at[k],
            recv_sem=gain_recv.at[k],
            device_id={"tm": lax.rem(m + k, n_tm)},
            device_id_type=MESH,
        )
        for k in range(1, n_tm)
    ]
    pending = spin_copies + gain_copies
    for copy in first_halo + pending:
        copy.start()

    for copy in spin_copies + gain_copies:
        copy.wait_recv()
    coefficients(own_full, 0)
    near_re = jnp.where(upper, spin_near[0, 0], spin_near[1, 0])
    near_im = jnp.where(upper, spin_near[0, 1], spin_near[1, 1])
    halo_full = powers(near_re, near_im, halo_re, halo_im)
    coefficients(halo_full, 1)

    limited = dup(flag_ref[...]) == 1

    for copy in first_halo:
        copy.wait_recv()
    for b in range(blocks):
        cur[rows(b), :] += halo_part(b)

    for sweep in range(SWEEPS):

        c = cur[...]
        c_sw = swap(c)
        c = c.reshape(ticks, blocks, width)
        c_sw = c_sw.reshape(ticks, blocks, width)
        cut = gain_in * clip_level
        scale = jnp.where(
            limited[None],
            cut[None] * lax.rsqrt(clip_level**2 + (c * c + c_sw * c_sw)),
            gain_in[None],
        )
        drive[...] = driven[...] - (scale * c).reshape(ticks * blocks, width)
        drive_sw[...] = driven_sw[...] - (scale * c_sw).reshape(ticks * blocks, width)

        def scan_step(t, carry):
            s, z = carry
            at = pl.ds(pl.multiple_of(t * blocks, blocks), blocks)
            g = gain_ref[t]
            a_re = g * spin_re
            a_im = g * spin_im
            new_s = a_re * s + (a_im * z + (drive[at, :]))
            new_z = a_re * z + (drive_sw[at, :] - a_im * s)
            scan_b[at, :] = new_s
            return new_s, new_z

        zero = jnp.zeros((blocks, width), jnp.float32)
        end_b, _ = lax.fori_loop(0, ticks, scan_step, (zero, zero), unroll=True)
        last = sweep == SWEEPS - 1
        ends[sweep, 0] = end_b
        end_copies = [
            pltpu.make_async_remote_copy(
                src_ref=ends.at[sweep, 0],
                dst_ref=ends.at[sweep, k],
                send_sem=end_send.at[sweep, k],
                recv_sem=end_recv.at[sweep, k],
                device_id={"tm": lax.rem(m + k, n_tm)},
                device_id_type=MESH,
            )
            for k in range(1, n_tm)
        ]
        near_copies = []
        halo_b = []
        if not last:
            near_copies = [
                pltpu.make_async_remote_copy(
                    src_ref=ends.at[sweep, 0],
                    dst_ref=ends_near.at[sweep, side, k],
                    send_sem=near_send.at[sweep, side, k],
                    recv_sem=near_recv.at[sweep, side, k],
                    device_id={"tm": lax.rem(m + k, n_tm), "region": sides[side]},
                    device_id_type=MESH,
                )
                for k in range(n_tm)
                for side in range(2)
            ]
            halo_b = halo_copies(sweep + 1, sent_b.at[sweep], got_b.at[sweep])
        for copy in end_copies + near_copies:
            copy.start()
        if not last:
            for b in range(blocks):
                sent_b[sweep, b] = scan_b[rows(b), :].astype(jnp.bfloat16)
            for copy in halo_b:
                copy.start()
        pending += end_copies + near_copies + halo_b

        def start_state(base, end_of):
            state = jnp.zeros((blocks, width), jnp.float32)
            for k in range(n_tm):
                v = end_of(k)
                state += coef[base, k, 0] * v + coef[base, k, 1] * swap(v)
            return state, swap(state)

        for copy in end_copies:
            copy.wait_recv()
        state, state_sw = start_state(0, lambda k: ends[sweep, k])
        if last:
            shape = (ticks, blocks, width)
            out = (
                pow_re[...].reshape(shape) * state[None]
                + pow_im[...].reshape(shape) * state_sw[None]
                + scan_b[...].reshape(shape)
            )
            out_ref[...] = out.reshape(ticks * blocks, width)
        else:
            if sweep == 0:
                for copy in first_halo:
                    copy.wait_send()
            for b in range(blocks):
                rounded[b] = (
                    pow_re[rows(b), :] * state[b : b + 1]
                    + pow_im[rows(b), :] * state_sw[b : b + 1]
                    + scan_b[rows(b), :]
                ).astype(jnp.bfloat16)
            for b in range(blocks):
                cur[rows(b), :] = own_part(b)
            for copy in near_copies:
                copy.wait_recv()
            state, state_sw = start_state(
                1,
                lambda k: jnp.where(upper, ends_near[sweep, 0, k], ends_near[sweep, 1, k]),
            )
            for copy in halo_b:
                copy.wait_recv()
            for b in range(blocks):
                halo[b] = (
                    halo_re[rows(b), :] * state[b : b + 1]
                    + halo_im[rows(b), :] * state_sw[b : b + 1]
                    + got_b[sweep, b].astype(jnp.float32)
                ).astype(jnp.bfloat16)
            for b in range(blocks):
                cur[rows(b), :] += halo_part(b)
    for copy in pending:
        copy.wait_send()


def local(n_tm, n_region, former, excitation, maps, target, attenuation, angle, flag, gain):
    ticks, blocks, width = former.shape
    flat = (ticks * blocks, width)
    f32, bf16 = jnp.float32, jnp.bfloat16
    rounds = SWEEPS - 1
    vmem = pl.BlockSpec(memory_space=pltpu.VMEM)
    hbm = pl.BlockSpec(memory_space=pl.ANY)
    dma = pltpu.SemaphoreType.DMA
    out = pl.pallas_call(
        functools.partial(kernel, n_tm, n_region, ticks, blocks),
        out_shape=jax.ShapeDtypeStruct(flat, f32),
        in_specs=[hbm] * 8,
        out_specs=vmem,
        scratch_shapes=[
            pltpu.SMEM(gain.shape, f32),
            pltpu.SMEM(target.shape[::-1], target.dtype),
            pltpu.VMEM(flat, f32),
            pltpu.VMEM(flat, bf16),
            pltpu.VMEM(maps.shape, bf16),
            pltpu.VMEM(attenuation.shape, f32),
            pltpu.VMEM(angle.shape, f32),
            pltpu.VMEM(flag.shape, flag.dtype),
            pltpu.VMEM((blocks, ticks, width), bf16),
            pltpu.VMEM((blocks, ticks, width), bf16),
            pltpu.VMEM((rounds, blocks, ticks, width), bf16),
            pltpu.VMEM((rounds, blocks, ticks, width), bf16),
            pltpu.VMEM(flat, f32),
            pltpu.VMEM(flat, f32),
            pltpu.VMEM(flat, f32),
            pltpu.VMEM(flat, f32),
            pltpu.VMEM(flat, f32),
            pltpu.VMEM(flat, f32),
            pltpu.VMEM(flat, f32),
            pltpu.VMEM(flat, f32),
            pltpu.VMEM(flat, f32),
            pltpu.VMEM(flat, f32),
            pltpu.VMEM((2, blocks, width), f32),
            pltpu.VMEM((2, 2, blocks, width), f32),
            pltpu.VMEM((n_tm, blocks, width), f32),
            pltpu.VMEM((SWEEPS, n_tm, blocks, width), f32),
            pltpu.VMEM((rounds, 2, n_tm, blocks, width), f32),
            pltpu.VMEM((2, n_tm, 4, blocks, width), f32),
            dma((SWEEPS, 2)),
            dma((SWEEPS, 2)),
            dma((2,)),
            dma((2,)),
            dma((n_tm,)),
            dma((n_tm,)),
            dma((SWEEPS, n_tm)),
            dma((SWEEPS, n_tm)),
            dma((rounds, 2, n_tm)),
            dma((rounds, 2, n_tm)),
            dma((8,)),
        ],
        compiler_params=pltpu.CompilerParams(
            collective_id=0, has_side_effects=True
        ),
        name="picard",
    )(
        gain,
        target.T,
        former.reshape(flat),
        excitation.reshape(flat),
        maps,
        attenuation,
        angle,
        flag,
    )
    return out.reshape(ticks, blocks, width)


def solution(mesh):
    in_specs = (
        P(("cases", "tm"), "region", None),
        P(("cases", "tm"), "region", None),
        P("region", None, None, None),
        P("region", None),
        P("region", None),
        P("region", None),
        P(("cases", "region"), None),
        P(("cases", "tm")),
    )
    return jax.shard_map(
        functools.partial(local, mesh.shape["tm"], mesh.shape["region"]),
        mesh=mesh,
        in_specs=in_specs,
        out_specs=P(("cases", "tm"), "region", None),
        check_vma=False,
    )
```

```python
import functools

import jax
import jax.numpy as jnp
from jax import lax
from jax.experimental import pallas as pl
from jax.experimental.pallas import tpu as pltpu
from jax.sharding import PartitionSpec as P

SWEEPS = 3
BND = 4
clip_level = 0.5
MESH = pl.DeviceIdType.MESH


def swap(v):
    return pltpu.roll(v, v.shape[-1] // 2, v.ndim - 1)


def dup(v):
    return jnp.concatenate([v, v], axis=-1)


def complex_pair(first, second):
    return (
        first[0] * second[0] - first[1] * second[1],
        first[0] * second[1] + first[1] * second[0],
    )


def dot_nt(x, w):
    return lax.dot_general(x, w, (((1,), (1,)), ((), ())), preferred_element_type=jnp.float32)


def kernel(
    n_tm,
    n_region,
    ticks,
    blocks,
    gain_hbm,
    target_hbm,
    former_hbm,
    exc_hbm,
    maps_hbm,
    att_hbm,
    angle_hbm,
    flag_hbm,
    out_ref,
    gain_ref,
    target_ref,
    former_ref,
    exc_ref,
    maps_ref,
    att_ref,
    angle_ref,
    flag_ref,
    rounded,
    halo,
    sent_b,
    got_b,
    cur,
    scan_b,
    pow_re,
    pow_im,
    halo_re,
    halo_im,
    driven,
    driven_sw,
    drive,
    drive_sw,
    spin,
    spin_near,
    gains,
    ends,
    ends_near,
    coef,
    halo_send,
    halo_recv,
    spin_send,
    spin_recv,
    gain_send,
    gain_recv,
    end_send,
    end_recv,
    near_send,
    near_recv,
    fetch_sem,
):
    m = lax.axis_index("tm")
    r = lax.axis_index("region")
    right = lax.rem(r + 1, n_region)
    left = lax.rem(r + n_region - 1, n_region)
    sides = (left, right)
    width = out_ref.shape[-1]

    def rows(b):
        return pl.ds(b, ticks, stride=blocks)

    fetches = [
        pltpu.make_async_copy(src, dst, fetch_sem.at[i])
        for i, (src, dst) in enumerate(
            (
                (former_hbm, former_ref),
                (att_hbm, att_ref),
                (angle_hbm, angle_ref),
                (gain_hbm, gain_ref),
                (target_hbm, target_ref),
                (maps_hbm, maps_ref),
                (exc_hbm, exc_ref),
                (flag_hbm, flag_ref),
            )
        )
    ]
    for fetch in fetches:
        fetch.start()
    barrier = pltpu.get_barrier_semaphore()
    for k in range(n_tm):
        rank = lax.rem(m + k, n_tm)
        for region in (left, right) if k == 0 else (r, left, right):
            pl.semaphore_signal(
                barrier, inc=1, device_id={"tm": rank, "region": region}, device_id_type=MESH
            )

    lane = lax.broadcasted_iota(jnp.int32, (blocks, width), 1)
    row = lax.broadcasted_iota(jnp.int32, (blocks, width), 0)
    sign = jnp.where(lane < width // 2, -1.0, 1.0)
    upper = row < BND

    fetches[0].wait()
    for b in range(blocks):
        rounded[b] = former_ref[rows(b), :].astype(jnp.bfloat16)
    for fetch in fetches[1:4]:
        fetch.wait()
    modulus = jnp.exp(-dup(att_ref[...]))
    angle = dup(angle_ref[...])
    cosine = modulus * jnp.cos(angle)
    sine = modulus * jnp.sin(angle)
    gain_in = jnp.sqrt((1.0 - cosine) ** 2 + sine**2)
    spin_re = cosine
    spin_im = sign * sine
    spin[0] = spin_re
    spin[1] = spin_im
    total_gain = lax.fori_loop(0, ticks, lambda t, q: q * gain_ref[t], jnp.float32(1.0))
    gains[0] = jnp.full((blocks, width), total_gain, jnp.float32)

    def partner(b, c):
        return lax.rem(target_ref[c, b], blocks)

    def own_part(b):
        x = jnp.concatenate([rounded[b], rounded[partner(b, 1)]], axis=1)
        return dot_nt(x, jnp.concatenate([maps_ref[b, 0], maps_ref[b, 1]], axis=1))

    def halo_part(b):
        x = jnp.concatenate([halo[partner(b, 2)], halo[partner(b, 3)]], axis=1)
        return dot_nt(x, jnp.concatenate([maps_ref[b, 2], maps_ref[b, 3]], axis=1))

    for fetch in fetches[4:]:
        fetch.wait()
    for b in range(blocks):
        cur[rows(b), :] = own_part(b)

    exc = exc_ref[...].astype(jnp.float32).reshape(ticks, blocks, width)
    exc = exc * gain_in[None]
    driven[...] = exc.reshape(ticks * blocks, width)
    driven_sw[...] = swap(driven[...])

    def powers(base_re, base_im, to_re, to_im):
        def step(t, carry):
            q, re, im = carry
            q = q * gain_ref[t]
            re, im = complex_pair((re, im), (base_re, base_im))
            at = pl.ds(pl.multiple_of(t * blocks, blocks), blocks)
            to_re[at, :] = q * re
            to_im[at, :] = q * im
            return q, re, im

        one = jnp.ones((blocks, width), jnp.float32)
        _, re, im = lax.fori_loop(
            0, ticks, step, (jnp.float32(1.0), one, jnp.zeros_like(one)), unroll=True
        )
        return re, im

    def coefficients(full, base):
        one = (jnp.ones((blocks, width), jnp.float32), jnp.zeros((blocks, width), jnp.float32))
        after, within = one, one
        for j in reversed(range(n_tm)):
            k = lax.rem(m - j + n_tm, n_tm)
            before = j < m
            factor = gains[k]
            end = (factor * full[0], factor * full[1])
            coef[base, k, 0] = after[0]
            coef[base, k, 1] = after[1]
            coef[base, k, 2] = jnp.where(before, within[0], 0.0)
            coef[base, k, 3] = jnp.where(before, within[1], 0.0)
            after = complex_pair(after, end)
            longer = complex_pair(within, end)
            within = tuple(jnp.where(before, a, b) for a, b in zip(longer, within))
        down = (1.0 - after[0], -after[1])
        square = down[0] ** 2 + down[1] ** 2
        head = complex_pair(within, (down[0] / square, -down[1] / square))
        for k in range(n_tm):
            c = complex_pair(head, (coef[base, k, 0], coef[base, k, 1]))
            coef[base, k, 0] = c[0] + coef[base, k, 2]
            coef[base, k, 1] = c[1] + coef[base, k, 3]

    own_full = powers(spin_re, spin_im, pow_re, pow_im)
    pl.semaphore_wait(barrier, 3 * n_tm - 1)

    def halo_copies(step, src, dst):
        return [
            pltpu.make_async_remote_copy(
                src_ref=src.at[pl.ds(start, BND)],
                dst_ref=dst.at[pl.ds(start, BND)],
                send_sem=halo_send.at[step, side],
                recv_sem=halo_recv.at[step, side],
                device_id={"region": sides[side]},
                device_id_type=MESH,
            )
            for side, start in ((0, 0), (1, blocks - BND))
        ]

    first_halo = halo_copies(0, rounded, halo)
    spin_copies = [
        pltpu.make_async_remote_copy(
            src_ref=spin,
            dst_ref=spin_near.at[side],
            send_sem=spin_send.at[side],
            recv_sem=spin_recv.at[side],
            device_id={"region": sides[side]},
            device_id_type=MESH,
        )
        for side in range(2)
    ]
    gain_copies = [
        pltpu.make_async_remote_copy(
            src_ref=gains.at[0],
            dst_ref=gains.at[k],
            send_sem=gain_send.at[k],
            recv_sem=gain_recv.at[k],
            device_id={"tm": lax.rem(m + k, n_tm)},
            device_id_type=MESH,
        )
        for k in range(1, n_tm)
    ]
    pending = spin_copies + gain_copies
    for copy in first_halo + pending:
        copy.start()

    limited = dup(flag_ref[...]) == 1

    for copy in first_halo:
        copy.wait_recv()
    for b in range(blocks):
        cur[rows(b), :] += halo_part(b)

    for sweep in range(SWEEPS):

        c = cur[...]
        c_sw = swap(c)
        c = c.reshape(ticks, blocks, width)
        c_sw = c_sw.reshape(ticks, blocks, width)
        cut = gain_in * clip_level
        scale = jnp.where(
            limited[None],
            cut[None] * lax.rsqrt(clip_level**2 + (c * c + c_sw * c_sw)),
            gain_in[None],
        )
        drive[...] = driven[...] - (scale * c).reshape(ticks * blocks, width)
        drive_sw[...] = driven_sw[...] - (scale * c_sw).reshape(ticks * blocks, width)

        def scan_step(t, carry):
            s, z = carry
            at = pl.ds(pl.multiple_of(t * blocks, blocks), blocks)
            g = gain_ref[t]
            a_re = g * spin_re
            a_im = g * spin_im
            new_s = a_re * s + (a_im * z + (drive[at, :]))
            new_z = a_re * z + (drive_sw[at, :] - a_im * s)
            scan_b[at, :] = new_s
            return new_s, new_z

        zero = jnp.zeros((blocks, width), jnp.float32)
        end_b, _ = lax.fori_loop(0, ticks, scan_step, (zero, zero), unroll=True)
        last = sweep == SWEEPS - 1
        ends[sweep, 0] = end_b
        end_copies = [
            pltpu.make_async_remote_copy(
                src_ref=ends.at[sweep, 0],
                dst_ref=ends.at[sweep, k],
                send_sem=end_send.at[sweep, k],
                recv_sem=end_recv.at[sweep, k],
                device_id={"tm": lax.rem(m + k, n_tm)},
                device_id_type=MESH,
            )
            for k in range(1, n_tm)
        ]
        near_copies = []
        halo_b = []
        if not last:
            near_copies = [
                pltpu.make_async_remote_copy(
                    src_ref=ends.at[sweep, 0],
                    dst_ref=ends_near.at[sweep, side, k],
                    send_sem=near_send.at[sweep, side, k],
                    recv_sem=near_recv.at[sweep, side, k],
                    device_id={"tm": lax.rem(m + k, n_tm), "region": sides[side]},
                    device_id_type=MESH,
                )
                for k in range(n_tm)
                for side in range(2)
            ]
            halo_b = halo_copies(sweep + 1, sent_b.at[sweep], got_b.at[sweep])
        for copy in end_copies + near_copies:
            copy.start()
        if not last:
            for b in range(blocks):
                sent_b[sweep, b] = scan_b[rows(b), :].astype(jnp.bfloat16)
            for copy in halo_b:
                copy.start()
        pending += end_copies + near_copies + halo_b

        if sweep == 0:
            for copy in spin_copies + gain_copies:
                copy.wait_recv()
            coefficients(own_full, 0)
            near_re = jnp.where(upper, spin_near[0, 0], spin_near[1, 0])
            near_im = jnp.where(upper, spin_near[0, 1], spin_near[1, 1])
            halo_full = powers(near_re, near_im, halo_re, halo_im)
            coefficients(halo_full, 1)

        def start_state(base, end_of):
            state = jnp.zeros((blocks, width), jnp.float32)
            for k in range(n_tm):
                v = end_of(k)
                state += coef[base, k, 0] * v + coef[base, k, 1] * swap(v)
            return state, swap(state)

        for copy in end_copies:
            copy.wait_recv()
        state, state_sw = start_state(0, lambda k: ends[sweep, k])
        if last:
            shape = (ticks, blocks, width)
            out = (
                pow_re[...].reshape(shape) * state[None]
                + pow_im[...].reshape(shape) * state_sw[None]
                + scan_b[...].reshape(shape)
            )
            out_ref[...] = out.reshape(ticks * blocks, width)
        else:
            if sweep == 0:
                for copy in first_halo:
                    copy.wait_send()
            for b in range(blocks):
                rounded[b] = (
                    pow_re[rows(b), :] * state[b : b + 1]
                    + pow_im[rows(b), :] * state_sw[b : b + 1]
                    + scan_b[rows(b), :]
                ).astype(jnp.bfloat16)
            for b in range(blocks):
                cur[rows(b), :] = own_part(b)
            for copy in near_copies:
                copy.wait_recv()
            state, state_sw = start_state(
                1,
                lambda k: jnp.where(upper, ends_near[sweep, 0, k], ends_near[sweep, 1, k]),
            )
            for copy in halo_b:
                copy.wait_recv()
            for b in range(blocks):
                halo[b] = (
                    halo_re[rows(b), :] * state[b : b + 1]
                    + halo_im[rows(b), :] * state_sw[b : b + 1]
                    + got_b[sweep, b].astype(jnp.float32)
                ).astype(jnp.bfloat16)
            for b in range(blocks):
                cur[rows(b), :] += halo_part(b)
    for copy in pending:
        copy.wait_send()


def local(n_tm, n_region, former, excitation, maps, target, attenuation, angle, flag, gain):
    ticks, blocks, width = former.shape
    flat = (ticks * blocks, width)
    f32, bf16 = jnp.float32, jnp.bfloat16
    rounds = SWEEPS - 1
    vmem = pl.BlockSpec(memory_space=pltpu.VMEM)
    hbm = pl.BlockSpec(memory_space=pl.ANY)
    dma = pltpu.SemaphoreType.DMA
    out = pl.pallas_call(
        functools.partial(kernel, n_tm, n_region, ticks, blocks),
        out_shape=jax.ShapeDtypeStruct(flat, f32),
        in_specs=[hbm] * 8,
        out_specs=vmem,
        scratch_shapes=[
            pltpu.SMEM(gain.shape, f32),
            pltpu.SMEM(target.shape[::-1], target.dtype),
            pltpu.VMEM(flat, f32),
            pltpu.VMEM(flat, bf16),
            pltpu.VMEM(maps.shape, bf16),
            pltpu.VMEM(attenuation.shape, f32),
            pltpu.VMEM(angle.shape, f32),
            pltpu.VMEM(flag.shape, flag.dtype),
            pltpu.VMEM((blocks, ticks, width), bf16),
            pltpu.VMEM((blocks, ticks, width), bf16),
            pltpu.VMEM((rounds, blocks, ticks, width), bf16),
            pltpu.VMEM((rounds, blocks, ticks, width), bf16),
            pltpu.VMEM(flat, f32),
            pltpu.VMEM(flat, f32),
            pltpu.VMEM(flat, f32),
            pltpu.VMEM(flat, f32),
            pltpu.VMEM(flat, f32),
            pltpu.VMEM(flat, f32),
            pltpu.VMEM(flat, f32),
            pltpu.VMEM(flat, f32),
            pltpu.VMEM(flat, f32),
            pltpu.VMEM(flat, f32),
            pltpu.VMEM((2, blocks, width), f32),
            pltpu.VMEM((2, 2, blocks, width), f32),
            pltpu.VMEM((n_tm, blocks, width), f32),
            pltpu.VMEM((SWEEPS, n_tm, blocks, width), f32),
            pltpu.VMEM((rounds, 2, n_tm, blocks, width), f32),
            pltpu.VMEM((2, n_tm, 4, blocks, width), f32),
            dma((SWEEPS, 2)),
            dma((SWEEPS, 2)),
            dma((2,)),
            dma((2,)),
            dma((n_tm,)),
            dma((n_tm,)),
            dma((SWEEPS, n_tm)),
            dma((SWEEPS, n_tm)),
            dma((rounds, 2, n_tm)),
            dma((rounds, 2, n_tm)),
            dma((8,)),
        ],
        compiler_params=pltpu.CompilerParams(
            collective_id=0, has_side_effects=True
        ),
        name="picard",
    )(
        gain,
        target.T,
        former.reshape(flat),
        excitation.reshape(flat),
        maps,
        attenuation,
        angle,
        flag,
    )
    return out.reshape(ticks, blocks, width)


def solution(mesh):
    in_specs = (
        P(("cases", "tm"), "region", None),
        P(("cases", "tm"), "region", None),
        P("region", None, None, None),
        P("region", None),
        P("region", None),
        P("region", None),
        P(("cases", "region"), None),
        P(("cases", "tm")),
    )
    return jax.shard_map(
        functools.partial(local, mesh.shape["tm"], mesh.shape["region"]),
        mesh=mesh,
        in_specs=in_specs,
        out_specs=P(("cases", "tm"), "region", None),
        check_vma=False,
    )
```
